32 devices in a mesh: dev: 32 (over z, y, x, core).
Axes of the slice: x: 2, y: 2, z: 4, core: 2. Of those that a mesh axis runs over, the one named last changes fastest.
Arguments:
- right_sides: float32 [32, 64, 512], P('dev'), may hold values from -6 to 6
- diag_inverse: float32 [64, 512, 512], P('dev'), may hold values from -0.25 to 0.25
- factor_tiles: float32 [256, 512, 512], P('dev'), may hold values from -0.09375 to 0.09375
- node_level: int32 [64], replicated, may hold values from 0 to 4, as said below
- tile_column: int32 [256], replicated, may hold values from 0 to 63, as said below
- tile_row: int32 [256], replicated, may hold values from 0 to 63, as said below
Outputs:
- solution: float32 [32, 64, 512], P('dev')
The draws below stay inside these ranges and needn't reach their ends.
Inputs may be any that keep to these rules, and one draw needn't show every extreme that they name: `node_level`: supernode s is owned by device s // 2; the 2 supernodes of one device lie at different levels, and every level holds supernodes of two or more devices. `tile_column`: tile k is held by device k // 8; its column supernode lies at a lower level than its row supernode. Among one device's tiles whose column supernodes lie at one level there are at most 4 tiles, 2 distinct column supernodes and 2 distinct row supernodes; some device reaches all three bounds. A pair of supernodes may recur on several tiles. `tile_row`: drawn together with tile_column, under its bounds.
All inputs are finite; a program needn't handle non-finite values.
Results may differ from the reference program's by a relative error of at most 0.0001.
Values sent between devices are 32-bit elements; how exact they have to be, the bound alone decides.
A program may use at most 128 MiB of HBM per device.

```python
import jax
import jax.numpy as jnp
from jax import lax

B = 512
SN_DEV = 2
TILE_DEV = 8
LEVELS = 5
R = 32
NS = 64
NT = 256


def build_tables(key):
    owners = NS // SN_DEV
    first_level = jnp.arange(owners, dtype=jnp.int32) % LEVELS
    advance = jax.random.randint(jax.random.fold_in(key, 101), (owners,), 1, LEVELS)
    second_level = (first_level + advance) % LEVELS
    node_level = jnp.stack([first_level, second_level], axis=1).reshape(-1).astype(jnp.int32)
    pattern = jax.random.randint(jax.random.fold_in(key, 102), (owners,), 0, 2)
    pattern = pattern.at[0].set(0)
    scores = jax.random.randint(jax.random.fold_in(key, 103), (owners, 4), 0, 1 << 20) * 4 + jnp.arange(4, dtype=jnp.int32)
    ranking = jnp.argsort(scores, axis=1, stable=True)
    base_counts = jnp.array([4, 2, 1, 1], dtype=jnp.int32)
    counts = jnp.where(pattern[:, None] == 0, base_counts[ranking], 2)
    end_slot = jnp.cumsum(counts, axis=1)
    start_slot = end_slot - counts
    slot_ids = jnp.arange(TILE_DEV, dtype=jnp.int32)
    group_level = jnp.sum((slot_ids[None, :, None] >= end_slot[:, None, :]).astype(jnp.int32), axis=2)
    group_start = jnp.take_along_axis(start_slot, group_level, axis=1)
    within_group = slot_ids[None, :] - group_start
    level_ids = jnp.arange(4, dtype=jnp.int32)
    node_ids = jnp.arange(NS, dtype=jnp.int32)

    def choose_two(salt_value, allowed):
        picks = jax.random.randint(jax.random.fold_in(key, salt_value), (owners, 4, NS), 0, 1 << 20) * NS + node_ids
        picks = jnp.where(allowed[None, :, :], picks, -1)
        return lax.top_k(picks, 2)[1].astype(jnp.int32)
    column_picks = choose_two(104, node_level[None, :] == level_ids[:, None])
    row_picks = choose_two(105, node_level[None, :] > level_ids[:, None])
    column = jnp.take_along_axis(column_picks.reshape(owners, 8), group_level * 2 + within_group % 2, axis=1)
    row = jnp.take_along_axis(row_picks.reshape(owners, 8), group_level * 2 + within_group // 2, axis=1)
    return (node_level, column.reshape(-1).astype(jnp.int32), row.reshape(-1).astype(jnp.int32))


def draw_node_level(key, part):
    return build_tables(key)[0]


def draw_tile_column(key, part):
    return build_tables(key)[1]


def draw_tile_row(key, part):
    return build_tables(key)[2]


def levels(own_key, dims, pieces, least, largest):
    factor_of, own = 1.0, jax.random.fold_in(own_key, 6)
    for axis_at, parts in pieces:
        draws = jnp.exp(jax.random.uniform(jax.random.fold_in(own, axis_at), (parts,), jnp.float32, least / len(pieces), largest / len(pieces)))
        factor_of = factor_of * jnp.repeat(draws, dims[axis_at] // parts).reshape([-1 if axis == axis_at else 1 for axis in range(len(dims))])
    return factor_of


def gaussian(rng, dims, spread, bound, cuts=(), held_as=jnp.bfloat16):
    drawn = spread * jax.random.normal(rng, dims, jnp.float32)
    if cuts:
        drawn = drawn * levels(rng, dims, cuts, -0.22, 0.18)
    return jnp.clip(drawn, -bound, bound).astype(held_as)


def setup_inputs(seed: int = 0) -> dict:
    keys = jax.random.split(jax.random.key(seed), 7)
    right_sides = gaussian(keys[0], (R, NS, B), 1.0, 6.0, ((0, 32),), jnp.float32)
    diag_inverse = gaussian(keys[1], (NS, B, B), B ** -0.5, 0.25, ((0, 32),), jnp.float32)
    factor_tiles = gaussian(keys[2], (NT, B, B), (8 * B) ** -0.5, 0.09375, ((0, 32),), jnp.float32)
    node_level = draw_node_level(jax.random.fold_in(keys[6], 71), 0)
    tile_column = draw_tile_column(jax.random.fold_in(keys[6], 71), 0)
    tile_row = draw_tile_row(jax.random.fold_in(keys[6], 71), 0)
    return dict(right_sides=right_sides, diag_inverse=diag_inverse, factor_tiles=factor_tiles, node_level=node_level, tile_column=tile_column, tile_row=tile_row)


full_precision = lax.Precision.HIGHEST


def reference(right_sides, diag_inverse, factor_tiles, node_level, tile_column, tile_row):
    tile_level = node_level[tile_column].astype(jnp.int32)
    ranking = jnp.argsort(tile_level, stable=True).astype(jnp.int32)
    solution = jnp.zeros_like(right_sides)
    update = jnp.zeros_like(right_sides)
    for current in range(LEVELS):
        solved = jnp.einsum('rsb,sbc->rsc', right_sides - update, diag_inverse, precision=full_precision)
        chosen = (node_level == current)[None, :, None]
        solution = jnp.where(chosen, solved, solution)
        first_tile = jnp.sum((tile_level < current).astype(jnp.int32)).astype(jnp.int32)
        last_tile = jnp.sum((tile_level <= current).astype(jnp.int32)).astype(jnp.int32)

        def apply_tile(position, partial_value, known=solution):
            tile_id = ranking[position]
            source = lax.dynamic_index_in_dim(known, tile_column[tile_id], 1, keepdims=False)
            term = jnp.dot(source, factor_tiles[tile_id], precision=full_precision, preferred_element_type=jnp.float32)
            target = lax.dynamic_index_in_dim(partial_value, tile_row[tile_id], 1, keepdims=False)
            return lax.dynamic_update_index_in_dim(partial_value, target + term, tile_row[tile_id], 1)

        update = lax.fori_loop(first_tile, last_tile, apply_tile, update)
    return solution
```

```python
import functools

import jax
import jax.numpy as jnp
from jax import lax
from jax.experimental import pallas as pl
from jax.experimental.pallas import tpu as pltpu
from jax.sharding import PartitionSpec as P

LEVELS = 5
TCAP = 4
MESH = pl.DeviceIdType.MESH
F32, BF16 = jnp.float32, jnp.bfloat16


def stack3(x):
    hi = x.astype(BF16)
    rest = x - hi.astype(F32)
    mid = rest.astype(BF16)
    lo = (rest - mid.astype(F32)).astype(BF16)
    return jnp.concatenate([hi, mid, lo], axis=0)


def dot(a, b):
    return jnp.dot(a, b, preferred_element_type=F32)


def kernel(n, tab, pick, drop, take, place, b_ref, dinv, tiles, out,
           stage, wh, wl, csplit, xsplit,
           s_res, r_res, s_sol, r_sol, s_car, r_car, s_pro, r_pro,
           load_sem, send_sem, recv_sem):
    me = lax.axis_index("dev")
    per_owner, per_holder = dinv.shape[0], tiles.shape[0]
    size = dinv.shape[1]

    loads = [pltpu.make_async_copy(dinv, stage.at[pl.ds(0, per_owner)], load_sem.at[0]),
             pltpu.make_async_copy(tiles, stage.at[pl.ds(per_owner, per_holder)], load_sem.at[1])]
    for c in loads:
        c.start()

    barrier = pltpu.get_barrier_semaphore()

    def greet(i, _):
        pl.semaphore_signal(barrier, inc=1, device_id=(lax.rem(me + i, n),), device_id_type=MESH)
        return 0

    lax.fori_loop(1, n, greet, 0)

    def begin(src, dst, k):
        def send(i, _):
            peer = lax.rem(me + i, n)
            pltpu.make_async_remote_copy(
                src_ref=src.at[peer], dst_ref=dst.at[me],
                send_sem=send_sem.at[k], recv_sem=recv_sem.at[k],
                device_id=(peer,), device_id_type=MESH).start()
            return 0

        lax.fori_loop(1, n, send, 0)
        dst[me] = src[me]

    def whole(src, dst, k):
        return pltpu.make_async_remote_copy(
            src_ref=src.at[pl.ds(0, n - 1)], dst_ref=dst.at[pl.ds(0, n - 1)],
            send_sem=send_sem.at[k], recv_sem=recv_sem.at[k],
            device_id=(lax.rem(me + 1, n),), device_id_type=MESH)

    def split(first, count):
        rows = 64
        per = size // rows

        def body(i, _):
            m, c = i // per, pl.multiple_of((i % per) * rows, rows)
            w = stage[first + m, pl.ds(c, rows), :]
            hi = w.astype(BF16)
            wh[first + m, pl.ds(c, rows), :] = hi
            wl[first + m, pl.ds(c, rows), :] = (w - hi.astype(F32)).astype(BF16)
            return 0

        lax.fori_loop(0, count * per, body, 0)

    def halves(x):
        hi = x.astype(BF16)
        return hi, (x - hi.astype(F32)).astype(BF16)

    def multiply(hi, lo, which):
        m = hi.shape[0]
        a = dot(jnp.concatenate([hi, lo], axis=0), wh[which])
        return a[:m] + a[m:] + dot(hi, wl[which])

    waits = []
    k = 0
    bsplit = stack3(b_ref[...])
    for level in range(LEVELS):
        res = dot(pick[level], bsplit)
        if level:
            width = 6 * n * level
            res = res - dot(drop[level, :, :width], csplit[:width])
        s_res[level] = res.reshape(n, 1, size)
        if level == 0:
            pl.semaphore_wait(barrier, n - 1)
        begin(s_res.at[level], r_res.at[level], k)
        if level == 0:
            loads[0].wait()
            split(0, per_owner)
        w = whole(s_res.at[level], r_res.at[level], k)
        w.wait_recv()
        waits.append(w)
        k += 1

        hi, lo = halves(r_res[level].reshape(n, size))
        s_sol[level] = multiply(hi, lo, tab[level]).reshape(n, 1, size)
        begin(s_sol.at[level], r_sol.at[level], k)
        if level == 0:
            loads[1].wait()
            split(per_owner, per_holder)
        w = whole(s_sol.at[level], r_sol.at[level], k)
        w.wait_recv()
        waits.append(w)
        k += 1

        xs = stack3(r_sol[level].reshape(n, size))
        xsplit[pl.ds(3 * n * level, 3 * n), :] = xs
        if level + 1 == LEVELS:
            break
        for j in range(2):
            s_car[level, :, j, :] = dot(take[level, j], xs)
        begin(s_car.at[level], r_car.at[level], k)
        w = whole(s_car.at[level], r_car.at[level], k)
        w.wait_recv()
        waits.append(w)
        k += 1

        sums = [jnp.zeros((n, size), F32), jnp.zeros((n, size), F32)]
        got = [r_car[level, :, j, :] for j in range(2)]
        for t in range(TCAP):
            at = LEVELS + (level * TCAP + t) * 4
            second = tab[at + 1].astype(F32)
            x = got[0] * (1.0 - second) + got[1] * second
            hi, lo = halves(x)
            y = multiply(hi, lo, tab[at])
            for j in range(2):
                sums[j] += y * tab[at + 2 + j].astype(F32)
        for j in range(2):
            s_pro[level, :, j, :] = sums[j]
        begin(s_pro.at[level], r_pro.at[level], k)
        w = whole(s_pro.at[level], r_pro.at[level], k)
        w.wait_recv()
        waits.append(w)
        k += 1
        for j in range(2):
            csplit[pl.ds(3 * n * (2 * level + j), 3 * n), :] = stack3(r_pro[level, :, j, :])

    out[...] = dot(place[...], xsplit[...])
    for w in waits:
        w.wait_send()


def plan(n, node_level, tile_column, tile_row, per_owner, per_holder):
    ns = node_level.shape[0]
    level_of = jnp.sum(jnp.where(tile_column[:, None] == jnp.arange(ns, dtype=jnp.int32), node_level, 0), axis=1)
    lev = level_of.reshape(n, per_holder)
    col, row = tile_column.reshape(n, per_holder), tile_row.reshape(n, per_holder)
    steps = jnp.arange(LEVELS - 1, dtype=jnp.int32)
    act = lev[None] == steps[:, None, None]
    ends = lambda v: jnp.stack([jnp.min(jnp.where(act, v, 1 << 20), axis=2),
                                jnp.max(jnp.where(act, v, -1), axis=2)], axis=1)
    cset, rset = ends(col), ends(row)
    dev = jnp.arange(n, dtype=jnp.int32)
    nodes = jnp.arange(ns, dtype=jnp.int32)
    every = jnp.arange(LEVELS, dtype=jnp.int32)
    owned = node_level.reshape(n, per_owner)
    hit = owned[None] == every[:, None, None]
    ids = nodes.reshape(n, per_owner)
    target = jnp.max(jnp.where(hit, ids, -7), axis=2)
    own_slot = jnp.max(jnp.where(hit, jnp.arange(per_owner, dtype=jnp.int32), 0), axis=2)
    take = (cset[..., None] // per_owner == dev).astype(BF16)
    take = jnp.tile(take, (1, 1, 1, 3))
    pick = (target[..., None] == nodes).astype(BF16)
    pick = jnp.tile(pick, (1, 1, 3))
    drop = (target[:, :, None, None, None] == rset[None, None]).astype(BF16)
    drop = jnp.tile(drop, (1, 1, 1, 1, 3)).reshape(LEVELS, n, -1)
    place = (nodes[:, None, None] // per_owner == dev) & (node_level[:, None, None] == every[None, :, None])
    place = jnp.tile(place.astype(BF16), (1, 1, 3)).reshape(ns, -1)

    me = lax.axis_index("dev")
    mine = lambda v: lax.dynamic_slice_in_dim(v, me * per_holder, per_holder, 0)
    mcol, mrow, mlev = mine(tile_column), mine(tile_row), mine(level_of)
    mact = mlev[None] == steps[:, None]
    order = jnp.arange(per_holder, dtype=jnp.int32)
    rank = jnp.sum((mact[:, None, :] & (order[None, :] < order[:, None])).astype(jnp.int32), axis=2)
    chosen = mact[:, None, :] & (rank[:, None, :] == jnp.arange(TCAP, dtype=jnp.int32)[None, :, None])
    c0 = jnp.min(jnp.where(mact, mcol, 1 << 20), axis=1)[:, None]
    r0 = jnp.min(jnp.where(mact, mrow, 1 << 20), axis=1)[:, None]
    pickv = lambda v: jnp.sum(jnp.where(chosen, v, 0), axis=2)
    slot = pickv(jnp.arange(per_holder, dtype=jnp.int32)[None, None, :]) + per_owner
    second = pickv((mcol[None] != c0).astype(jnp.int32)[:, None, :])
    w0 = pickv((mrow[None] == r0).astype(jnp.int32)[:, None, :])
    w1 = pickv((mrow[None] != r0).astype(jnp.int32)[:, None, :])
    table = jnp.stack([slot, second, w0, w1], axis=2).reshape(-1)
    own = lax.dynamic_index_in_dim(own_slot, me, 1, keepdims=False)
    return jnp.concatenate([own, table]), pick, drop, take, place


def per_device(right_sides, diag_inverse, factor_tiles, node_level, tile_column, tile_row):
    n = lax.axis_size("dev")
    per_owner, size = diag_inverse.shape[0], diag_inverse.shape[1]
    per_holder = factor_tiles.shape[0]
    ns = right_sides.shape[1]
    tab, pick, drop, take, place = plan(n, node_level, tile_column, tile_row, per_owner, per_holder)
    mats = per_owner + per_holder
    steps = LEVELS - 1
    phases = 2 * LEVELS + 2 * steps
    vmem = pl.BlockSpec(memory_space=pltpu.VMEM)
    hbm = pl.BlockSpec(memory_space=pl.ANY)
    one = pltpu.VMEM((LEVELS, n, 1, size), F32)
    two = pltpu.VMEM((steps, n, 2, size), F32)
    out = pl.pallas_call(
        functools.partial(kernel, n),
        out_shape=jax.ShapeDtypeStruct((ns, size), F32),
        in_specs=[pl.BlockSpec(memory_space=pltpu.SMEM), vmem, vmem, vmem, vmem, vmem, hbm, hbm],
        out_specs=vmem,
        scratch_shapes=[
            pltpu.VMEM((mats, size, size), F32),
            pltpu.VMEM((mats, size, size), BF16),
            pltpu.VMEM((mats, size, size), BF16),
            pltpu.VMEM((steps * 6 * n, size), BF16),
            pltpu.VMEM((LEVELS * 3 * n, size), BF16),
            one, one, one, one, two, two, two, two,
            pltpu.SemaphoreType.DMA((2,)),
            pltpu.SemaphoreType.DMA((phases,)),
            pltpu.SemaphoreType.DMA((phases,)),
        ],
        compiler_params=pltpu.CompilerParams(
            collective_id=0, has_side_effects=True, vmem_limit_bytes=60 * 1024 * 1024),
    )(tab, pick, drop, take, place, right_sides[0], diag_inverse, factor_tiles)
    return out[None]


def solution(mesh):
    placed = (P("dev", None, None), P("dev", None, None), P("dev", None, None), P(), P(), P())
    return jax.shard_map(
        per_device, mesh=mesh, in_specs=placed, out_specs=P("dev", None, None), check_vma=False
    )
```
